32 devices in a mesh: segment: 4 (over y, x), tensor: 4 (over z), dp: 2 (over core).
Axes of the slice: x: 2, y: 2, z: 4, core: 2. Of those that a mesh axis runs over, the one named last changes fastest.
Arguments:
- tokens: bfloat16 [2, 256, 8192], P('dp', 'tensor'), may hold values from -6 to 6
- cotangent: bfloat16 [2, 256, 8192], P('dp', 'tensor'), may hold values from -1.1953125 to 1.1953125
- sequence_job: int32 [2], P('dp'), may hold values from 0 to 31
- section_layer_list: int32 [4], replicated, may hold values from 0 to 1, as said below
- section_norm_gain: bfloat16 [4, 8192], P('segment'), may hold values from 0.099609375 to 1.8984375
- query_matrix: bfloat16 [4, 8192, 4096], P('segment', None, 'tensor'), may hold values from -0.0625 to 0.0625
- key_matrix: bfloat16 [4, 8192, 512], P('segment', None, 'tensor'), may hold values from -0.0625 to 0.0625
- value_matrix: bfloat16 [4, 8192, 512], P('segment', None, 'tensor'), may hold values from -0.0625 to 0.0625
- output_matrix: bfloat16 [4, 4096, 8192], P('segment', 'tensor'), may hold values from -0.09375 to 0.09375
- adapter_down_all: bfloat16 [4, 8192, 512], P('segment', 'tensor'), may hold values from -0.0625 to 0.0625
- adapter_up_all: bfloat16 [4, 512, 4096], P('segment', None, 'tensor'), may hold values from -0.09375 to 0.09375
Outputs:
- grad_down: float32 [4, 8192, 512], P('segment', 'tensor')
- grad_up: float32 [4, 512, 4096], P('segment', None, 'tensor')
The draws below stay inside these ranges and needn't reach their ends.
Inputs may be any that keep to these rules, and one draw needn't show every extreme that they name: `section_layer_list`: at least one section applies no layer and at least one applies one; each of the others applies none or one.
All inputs are finite; a program needn't handle non-finite values.
Results may differ from the reference program's by a relative error of at most 0.035.
Values may be sent and summed in bfloat16 or wider, within the bound.
No kernel may reach another device: no remote copies, remote signals or barrier semaphores. Data moves between devices by JAX's collectives and lax.ppermute only.
A program may use at most 192 MiB of HBM per device.

```python
import math
import jax
import jax.numpy as jnp
from jax import lax

MODEL_WIDTH = 8192
QUERY_HEADS = 32
KV_HEADS = 4
HEAD_SIZE = 128
ADAPTER_RANK = 16
ADAPTER_JOBS = 32
SEQUENCE_TOKENS = 256
NBLK = 2
N_SEGMENT = 4
N_TENSOR = 4


def draw_section_layer_list(key, part):
    bit_key = jax.random.fold_in(key, 11)
    order_key = jax.random.fold_in(key, 23)
    bits = jax.random.randint(bit_key, (N_SEGMENT,), 0, 2, dtype=jnp.int32)
    order = jax.random.permutation(order_key, N_SEGMENT)
    bits = bits.at[order[0]].set(0)
    bits = bits.at[order[1]].set(1)
    return bits.astype(jnp.int32)


def steps_of(stream_key, shape, pieces, low, top_value):
    gain, own = 1.0, jax.random.fold_in(stream_key, 6)
    for axis_at, shards_of in pieces:
        steps = jnp.exp(jax.random.uniform(jax.random.fold_in(own, axis_at), (shards_of,), jnp.float32, low / len(pieces), top_value / len(pieces)))
        gain = gain * jnp.repeat(steps, shape[axis_at] // shards_of).reshape([-1 if axis == axis_at else 1 for axis in range(len(shape))])
    return gain


def bell_draw(key, extent, width, most, shards=(), kind=jnp.bfloat16):
    entries = width * jax.random.normal(key, extent, jnp.float32)
    if shards:
        entries = entries * steps_of(key, extent, shards, -0.22, 0.18)
    return jnp.clip(entries, -most, most).astype(kind)


def setup_inputs(seed: int = 0) -> dict:
    key_list = jax.random.split(jax.random.key(seed), 12)
    return {
        "tokens": bell_draw(key_list[0], (NBLK, SEQUENCE_TOKENS, MODEL_WIDTH), 1.0, 6.0, ((0, 2), (1, 4))),
        "cotangent": bell_draw(key_list[1], (NBLK, SEQUENCE_TOKENS, MODEL_WIDTH), 0.2, 1.1953125, ((0, 2), (1, 4))),
        "sequence_job": jax.random.randint(key_list[2], (NBLK,), 0, ADAPTER_JOBS).astype(jnp.int32),
        "section_layer_list": draw_section_layer_list(jax.random.fold_in(key_list[11], 71), 0),
        "section_norm_gain": jnp.clip(1.0 + 0.18 * jax.random.normal(key_list[4], (N_SEGMENT, MODEL_WIDTH), jnp.float32), 0.099609375, 1.8984375).astype(jnp.bfloat16),
        "query_matrix": bell_draw(key_list[5], (N_SEGMENT, MODEL_WIDTH, QUERY_HEADS * HEAD_SIZE), MODEL_WIDTH ** -0.5, 0.0625, ((0, 4), (2, 4))),
        "key_matrix": bell_draw(key_list[6], (N_SEGMENT, MODEL_WIDTH, KV_HEADS * HEAD_SIZE), MODEL_WIDTH ** -0.5, 0.0625, ((0, 4), (2, 4))),
        "value_matrix": bell_draw(key_list[7], (N_SEGMENT, MODEL_WIDTH, KV_HEADS * HEAD_SIZE), MODEL_WIDTH ** -0.5, 0.0625, ((0, 4), (2, 4))),
        "output_matrix": bell_draw(key_list[8], (N_SEGMENT, QUERY_HEADS * HEAD_SIZE, MODEL_WIDTH), (QUERY_HEADS * HEAD_SIZE) ** -0.5, 0.09375, ((0, 4), (1, 4))),
        "adapter_down_all": bell_draw(key_list[9], (N_SEGMENT, MODEL_WIDTH, ADAPTER_JOBS * ADAPTER_RANK), MODEL_WIDTH ** -0.5, 0.0625, ((0, 4), (1, 4))),
        "adapter_up_all": bell_draw(key_list[10], (N_SEGMENT, ADAPTER_JOBS * ADAPTER_RANK, QUERY_HEADS * HEAD_SIZE), (QUERY_HEADS * HEAD_SIZE) ** -0.5, 0.09375, ((0, 4), (2, 4))),
    }


ADAPTER_SCALE = 2.0
EPSILON = 1e-05

def rotate(inputs, head_count):
    sequence_count, row_count, width_all = inputs.shape
    head_dim = width_all // head_count
    half_dim = head_dim // 2
    shaped = inputs.reshape(sequence_count, row_count, head_count, head_dim)
    positions = jnp.arange(row_count, dtype=jnp.float32)
    exponent = jnp.arange(half_dim, dtype=jnp.float32) * (2.0 / head_dim)
    frequency = jnp.exp(-math.log(10000.0) * exponent)
    angles = positions[:, None] * frequency[None, :]
    cosine_table = jnp.cos(angles)[None, :, None, :]
    sine_table = jnp.sin(angles)[None, :, None, :]
    first_half = shaped[..., :half_dim]
    second_half = shaped[..., half_dim:]
    turned = jnp.concatenate([first_half * cosine_table - second_half * sine_table, second_half * cosine_table + first_half * sine_table], axis=-1)
    return turned.reshape(sequence_count, row_count, width_all)

def attend(query_rows, key_rows, value_rows, head_dim):
    sequence_count, row_count, query_span_width = query_rows.shape
    head_count = query_span_width // head_dim
    key_heads = key_rows.shape[-1] // head_dim
    group_size = head_count // key_heads
    rotated_queries = rotate(query_rows, head_count).reshape(sequence_count, row_count, key_heads, group_size, head_dim)
    rotated_keys = rotate(key_rows, key_heads).reshape(sequence_count, row_count, key_heads, head_dim)
    value_heads = value_rows.reshape(sequence_count, row_count, key_heads, head_dim)
    scores = jnp.einsum('bqhgd,bshd->bhgqs', rotated_queries, rotated_keys) / math.sqrt(head_dim)
    causal = jnp.arange(row_count)[:, None] >= jnp.arange(row_count)[None, :]
    scores = jnp.where(causal, scores, -1e+30)
    weights = jnp.exp(scores)
    probability = weights / lax.optimization_barrier(jnp.sum(weights, axis=-1, keepdims=True))
    output = jnp.einsum('bhgqs,bshd->bqhgd', probability, value_heads)
    return output.reshape(sequence_count, row_count, query_span_width)

def reference(tokens, cotangent, sequence_job, section_layer_list, section_norm_gain, query_matrix, key_matrix, value_matrix, output_matrix, adapter_down_all, adapter_up_all):
    sequence_count = tokens.shape[0]
    query_span_width = QUERY_HEADS * HEAD_SIZE
    key_width = KV_HEADS * HEAD_SIZE
    q_cols = query_span_width // N_TENSOR
    k_cols = key_width // N_TENSOR
    width_columns = MODEL_WIDTH // N_TENSOR
    onehot = (sequence_job[:, None] == jnp.arange(ADAPTER_JOBS, dtype=jnp.int32)[None, :]).astype(jnp.float32)
    hidden = tokens
    stored = []
    for relay_section in range(N_SEGMENT):
        stream = hidden.astype(jnp.float32)
        inverse = lax.rsqrt(lax.optimization_barrier(jnp.mean(stream * stream, axis=-1, keepdims=True)) + EPSILON)
        gain_row = section_norm_gain[relay_section].astype(jnp.float32)
        normed = (stream * inverse * gain_row).astype(jnp.bfloat16)
        flattened_rows = normed.reshape(sequence_count * SEQUENCE_TOKENS, MODEL_WIDTH)
        query_rows = jnp.dot(flattened_rows, query_matrix[relay_section], preferred_element_type=jnp.float32).reshape(sequence_count, SEQUENCE_TOKENS, query_span_width)
        key_rows = jnp.dot(flattened_rows, key_matrix[relay_section], preferred_element_type=jnp.float32).reshape(sequence_count, SEQUENCE_TOKENS, key_width)
        value_rows = jnp.dot(flattened_rows, value_matrix[relay_section], preferred_element_type=jnp.float32).reshape(sequence_count, SEQUENCE_TOKENS, key_width)
        every_job = jnp.dot(flattened_rows, adapter_down_all[relay_section], preferred_element_type=jnp.float32).reshape(sequence_count, SEQUENCE_TOKENS, ADAPTER_JOBS, ADAPTER_RANK)
        reduced_rank = lax.optimization_barrier(jnp.sum(every_job * onehot[:, None, :, None], axis=2))
        picked_up = adapter_up_all[relay_section].reshape(ADAPTER_JOBS, ADAPTER_RANK, query_span_width)[sequence_job].astype(jnp.float32)
        query_rows = query_rows + ADAPTER_SCALE * jnp.einsum('aqw,awy->aqy', reduced_rank, picked_up)
        attended = attend(query_rows, key_rows, value_rows, HEAD_SIZE).astype(jnp.bfloat16)
        flat_attended = attended.reshape(sequence_count * SEQUENCE_TOKENS, query_span_width)
        summed = jnp.zeros((sequence_count * SEQUENCE_TOKENS, MODEL_WIDTH), jnp.float32)
        for member in range(N_TENSOR):
            partial_addend = jnp.dot(flat_attended[:, member * q_cols:(member + 1) * q_cols], output_matrix[relay_section][member * q_cols:(member + 1) * q_cols], preferred_element_type=jnp.float32)
            summed = summed + lax.optimization_barrier(partial_addend.astype(jnp.bfloat16)).astype(jnp.float32)
        updated = (stream + summed.reshape(sequence_count, SEQUENCE_TOKENS, MODEL_WIDTH)).astype(jnp.bfloat16)
        applies = section_layer_list[relay_section] > 0
        stored.append((stream, inverse, normed, query_rows, key_rows, value_rows, reduced_rank, picked_up))
        hidden = jnp.where(applies, updated, hidden)
    gradient = cotangent.astype(jnp.float32)
    grads_down = [None] * N_SEGMENT
    grads_up = [None] * N_SEGMENT
    for relay_section in reversed(range(N_SEGMENT)):
        stream, inverse, normed, query_rows, key_rows, value_rows, reduced_rank, picked_up = stored[relay_section]
        applies = section_layer_list[relay_section] > 0
        flat_grad = gradient.astype(jnp.bfloat16).reshape(sequence_count * SEQUENCE_TOKENS, MODEL_WIDTH)
        grad_attended = jnp.dot(flat_grad, output_matrix[relay_section].T, preferred_element_type=jnp.float32).reshape(sequence_count, SEQUENCE_TOKENS, query_span_width)
        unused, pullback = jax.vjp(lambda first_in, second_in, third_in: attend(first_in, second_in, third_in, HEAD_SIZE), query_rows, key_rows, value_rows)
        query_gradient, key_gradient, value_gradient = pullback(grad_attended)
        shared_up_adapter = ADAPTER_SCALE * jnp.einsum('mxh,mxi->mhi', reduced_rank, query_gradient)
        grad_up = jnp.einsum('bj,bkc->jkc', onehot, shared_up_adapter).reshape(ADAPTER_JOBS * ADAPTER_RANK, query_span_width)
        reduced_gradient = ADAPTER_SCALE * jnp.einsum('ehy,ety->eht', query_gradient, picked_up)
        share_down = jnp.einsum('brd,brk->bdk', normed.astype(jnp.float32), reduced_gradient)
        grad_down = jnp.einsum('bj,bdk->djk', onehot, share_down).reshape(MODEL_WIDTH, ADAPTER_JOBS * ADAPTER_RANK)
        picked_down = adapter_down_all[relay_section].reshape(MODEL_WIDTH, ADAPTER_JOBS, ADAPTER_RANK)[:, sequence_job, :].astype(jnp.float32)
        query_bf = query_gradient.astype(jnp.bfloat16).reshape(sequence_count * SEQUENCE_TOKENS, query_span_width)
        keys_bf = key_gradient.astype(jnp.bfloat16).reshape(sequence_count * SEQUENCE_TOKENS, key_width)
        values_bf = value_gradient.astype(jnp.bfloat16).reshape(sequence_count * SEQUENCE_TOKENS, key_width)
        grad_norm = jnp.zeros((sequence_count * SEQUENCE_TOKENS, MODEL_WIDTH), jnp.float32)
        for member in range(N_TENSOR):
            q_low, q_high = (member * q_cols, (member + 1) * q_cols)
            k_low, k_high = (member * k_cols, (member + 1) * k_cols)
            width_lower, width_upper = (member * width_columns, (member + 1) * width_columns)
            partial_addend = jnp.dot(query_bf[:, q_low:q_high], query_matrix[relay_section][:, q_low:q_high].T, preferred_element_type=jnp.float32)
            partial_addend = partial_addend + jnp.dot(keys_bf[:, k_low:k_high], key_matrix[relay_section][:, k_low:k_high].T, preferred_element_type=jnp.float32)
            partial_addend = partial_addend + jnp.dot(values_bf[:, k_low:k_high], value_matrix[relay_section][:, k_low:k_high].T, preferred_element_type=jnp.float32)
            adapter_addend = jnp.einsum('hem,uhm->heu', reduced_gradient, picked_down[width_lower:width_upper]).reshape(sequence_count * SEQUENCE_TOKENS, width_columns)
            partial_addend = partial_addend.at[:, width_lower:width_upper].add(adapter_addend)
            grad_norm = grad_norm + lax.optimization_barrier(partial_addend.astype(jnp.bfloat16)).astype(jnp.float32)
        grad_norm = grad_norm.reshape(sequence_count, SEQUENCE_TOKENS, MODEL_WIDTH)
        gained = grad_norm * section_norm_gain[relay_section].astype(jnp.float32)
        grad_hidden = inverse * gained - stream * inverse ** 3 * lax.optimization_barrier(jnp.mean(gained * stream, axis=-1, keepdims=True))
        gradient = jnp.where(applies, gradient + grad_hidden, gradient)
        grads_down[relay_section] = jnp.where(applies, grad_down, jnp.zeros_like(grad_down))
        grads_up[relay_section] = jnp.where(applies, grad_up, jnp.zeros_like(grad_up))
        gradient = lax.optimization_barrier(gradient.astype(jnp.bfloat16)).astype(jnp.float32)
    return (jnp.stack(grads_down), jnp.stack(grads_up))
```

```python
import math

import jax
import jax.numpy as jnp
from jax import lax
from jax.sharding import PartitionSpec as P

HEAD_SIZE = 128
ADAPTER_RANK = 16
ADAPTER_JOBS = 32
ADAPTER_SCALE = 2.0
EPSILON = 1e-05

S, T, D = "segment", "tensor", "dp"
FEW = 4


def put(buffer, block, index):
    return lax.dynamic_update_slice_in_dim(buffer, block[None], index, 0)


def pick(stack, index):
    return lax.dynamic_index_in_dim(stack, index, 0, keepdims=False)


def rolled(block, columns, distance):
    nz = lax.axis_size(T)
    route = [(c * nz + z, c * nz + (z + distance) % nz) for c in columns for z in range(nz)]
    return lax.ppermute(block, (S, T), route)


def across(block, moves):
    nz = lax.axis_size(T)
    return lax.ppermute(block, (S, T), [(a * nz + z, b * nz + z) for a, b in moves for z in range(nz)])


def tensor_sum(stack, columns):
    nz, zi = lax.axis_size(T), lax.axis_index(T)
    total = pick(stack, zi).astype(jnp.float32)
    for r in range(1, nz):
        total = total + rolled(pick(stack, (zi + r) % nz), columns, r).astype(jnp.float32)
    return total.astype(stack.dtype)


def tensor_gather(block, columns):
    nz, zi = lax.axis_size(T), lax.axis_index(T)
    buffer = put(jnp.zeros((nz,) + block.shape, block.dtype), block, zi)
    for r in range(1, nz):
        buffer = put(buffer, rolled(block, columns, r), (zi - r) % nz)
    return buffer


def hop(partial, source, target):
    nz, me = lax.axis_size(T), lax.axis_index(S)
    rows, width = partial.shape
    groups = partial.reshape(nz, 4, rows // (4 * nz), width)
    to_x = across(groups[:, 2], [(source, source ^ 1)])
    to_y = across(groups[:, 3], [(source, source ^ 2)])
    own = tensor_sum(groups[:, 0:2], [source])
    one = tensor_sum(jnp.where(me == (source ^ 1), to_x, to_y), [source ^ 1, source ^ 2])
    if source ^ target == 3:
        by_x = across(jnp.where(me == source, own[1], one), [(source, target ^ 2), (target ^ 1, target)])
        by_y = across(jnp.where(me == source, own[0], one), [(source, target ^ 1), (target ^ 2, target)])
        pair = jnp.stack([by_y, by_x])
        single = jnp.where(me == (target ^ 2), by_x, by_y)
    else:
        rest = 3 - (source ^ target)
        got = across(jnp.where(me == source, own[1], one), [(source, target), (source ^ rest, target ^ rest)])
        pair = jnp.stack([got, one])
        single = jnp.where(me == source, own[0], got)
    gathered = tensor_gather(single, [target ^ 1, target ^ 2])
    from_x = across(gathered, [(target ^ 1, target)])
    from_y = across(gathered, [(target ^ 2, target)])
    two = tensor_gather(pair, [target])
    if source ^ target == 1:
        parts = [from_x, two[:, 0], two[:, 1], from_y]
    elif source ^ target == 2:
        parts = [from_y, two[:, 0], from_x, two[:, 1]]
    else:
        parts = [from_x, from_y, two[:, 0], two[:, 1]]
    return jnp.stack(parts, axis=1).reshape(rows, width)


def plain_hop(partial, source, target):
    shard = lax.psum_scatter(partial, T, scatter_dimension=0, tiled=True)
    shard = across(shard, [(source, target)])
    return lax.all_gather(shard, T, axis=0, tiled=True)


def spread(block):
    n, nz = lax.axis_size(S), lax.axis_size(T)
    me = lax.axis_index(S)
    rows, width = block.shape
    if n != 4 or width % 2048 or nz % 2 or nz > FEW:
        return lax.all_gather(block, T, axis=0, tiled=True)
    unit = width // 16 * 3
    first = width - 4 * unit
    mine = tensor_gather(lax.dynamic_slice_in_dim(block, first + me * unit, unit, 1), range(n))
    half = nz // 2
    x_swap = [(c, c ^ 1) for c in range(n)]
    y_swap = [(c, c ^ 2) for c in range(n)]
    by_x = across(mine, x_swap)
    by_y = across(mine, y_swap)
    far_low = across(by_y[:half], x_swap)
    far_high = across(by_x[half:], y_swap)
    block, unused = lax.optimization_barrier((block, mine))
    base = tensor_gather(block[:, :first], range(n))
    out = jnp.zeros((nz, rows, width), block.dtype)
    out = lax.dynamic_update_slice(out, base, (0, 0, 0))
    for piece, column, z in (
        (mine, me, 0),
        (by_x, me ^ 1, 0),
        (by_y, me ^ 2, 0),
        (far_low, me ^ 3, 0),
        (far_high, me ^ 3, half),
    ):
        out = lax.dynamic_update_slice(out, piece, (z, 0, first + column * unit))
    return out.reshape(nz * rows, width)


def swapped(block, bit):
    count = lax.axis_size(T)
    return lax.ppermute(block, T, [(i, i ^ 1 << bit) for i in range(count)])


def tensor_total(block):
    nz = lax.axis_size(T)
    if nz & (nz - 1):
        return lax.psum(block, T)
    for bit in range(nz.bit_length() - 1):
        block = block + swapped(block, bit)
    return block


def rotate(inputs, head_count):
    row_count, width_all = inputs.shape
    head_dim = width_all // head_count
    half_dim = head_dim // 2
    shaped = inputs.reshape(row_count, head_count, head_dim)
    positions = jnp.arange(row_count, dtype=jnp.float32)
    exponent = jnp.arange(half_dim, dtype=jnp.float32) * (2.0 / head_dim)
    frequency = jnp.exp(-math.log(10000.0) * exponent)
    angles = positions[:, None] * frequency[None, :]
    cosine_table = jnp.cos(angles)[:, None, :]
    sine_table = jnp.sin(angles)[:, None, :]
    first_half = shaped[..., :half_dim]
    second_half = shaped[..., half_dim:]
    turned = jnp.concatenate(
        [
            first_half * cosine_table - second_half * sine_table,
            second_half * cosine_table + first_half * sine_table,
        ],
        axis=-1,
    )
    return turned.reshape(row_count, width_all)


def attend(query_rows, key_rows, value_rows):
    row_count, query_width = query_rows.shape
    head_count = query_width // HEAD_SIZE
    key_heads = key_rows.shape[-1] // HEAD_SIZE
    rotated_queries = rotate(query_rows, head_count).reshape(row_count, key_heads, -1, HEAD_SIZE)
    rotated_keys = rotate(key_rows, key_heads).reshape(row_count, key_heads, HEAD_SIZE)
    value_heads = value_rows.reshape(row_count, key_heads, HEAD_SIZE)
    scores = jnp.einsum("qhgd,shd->hgqs", rotated_queries, rotated_keys) / math.sqrt(HEAD_SIZE)
    causal = jnp.arange(row_count)[:, None] >= jnp.arange(row_count)[None, :]
    scores = jnp.where(causal, scores, -1e30)
    weights = jnp.exp(scores)
    probability = weights / jnp.sum(weights, axis=-1, keepdims=True)
    output = jnp.einsum("hgqs,shd->qhgd", probability, value_heads)
    return output.reshape(row_count, query_width)


def dot(a, b, dims=((1,), (0,))):
    return lax.dot_general(a, b, (dims, ((), ())), preferred_element_type=jnp.float32)


def sequence_gradients(tokens, cotangent, job, sections, gain, weights, adapters):
    query_weight, key_weight, value_weight, out_weight = weights
    down_adapter, up_adapter = adapters
    n, nz = lax.axis_size(S), lax.axis_size(T)
    me, zi = lax.axis_index(S), lax.axis_index(T)
    local_rows, width = tokens.shape
    rows = local_rows * nz
    piece_width = down_adapter.shape[0]
    key_local = key_weight.shape[1]
    bits = (HEAD_SIZE // key_local).bit_length() - 1 if key_local < HEAD_SIZE else 0
    count, order, applies = sections

    picked_down = lax.dynamic_slice_in_dim(down_adapter, job * ADAPTER_RANK, ADAPTER_RANK, 1)
    if nz > FEW:
        picked_down = lax.all_gather(picked_down, T, axis=0, tiled=True)
    else:
        picked_down = tensor_gather(picked_down, range(n)).reshape(width, ADAPTER_RANK)
    picked_up = lax.dynamic_slice_in_dim(up_adapter, job * ADAPTER_RANK, ADAPTER_RANK, 0)
    here = (jnp.arange(rows) // local_rows == zi)[:, None]

    def low_side(bit):
        return zi // 2**bit % 2 == 0

    def share_heads(block):
        for bit in range(bits):
            other = swapped(block.astype(jnp.bfloat16), bit).astype(block.dtype)
            block = jnp.where(
                low_side(bit), jnp.concatenate([block, other], -1), jnp.concatenate([other, block], -1)
            )
        return block

    def split_back(block):
        for bit in reversed(range(bits)):
            half = block.shape[-1] // 2
            keep = jnp.where(low_side(bit), block[:, :half], block[:, half:])
            send = jnp.where(low_side(bit), block[:, half:], block[:, :half])
            block = keep + swapped(send.astype(jnp.bfloat16), bit).astype(block.dtype)
        return block

    def forward(hidden):
        stream = hidden.astype(jnp.float32)
        inverse = lax.rsqrt(jnp.mean(stream * stream, axis=-1, keepdims=True) + EPSILON)
        normed = (stream * inverse * gain).astype(jnp.bfloat16)
        low_rank = dot(normed, picked_down)
        queries = dot(normed, query_weight) + ADAPTER_SCALE * dot(low_rank, picked_up.astype(jnp.float32))
        key_own, value_own = dot(normed, key_weight), dot(normed, value_weight)
        keys, values = share_heads(key_own), share_heads(value_own)
        return hidden, inverse, normed, low_rank, queries, keys, values, key_own, value_own

    def project_out(state):
        attended = attend(state[4], state[5], state[6]).astype(jnp.bfloat16)
        return (dot(attended, out_weight) + jnp.where(here, state[0], 0).astype(jnp.float32)).astype(jnp.bfloat16)

    def backward(grad, state):
        queries, keys, values = state[4:7]
        grad_attended = dot(grad, out_weight, ((1,), (1,)))
        unused, pullback = jax.vjp(attend, queries, keys, values)
        grad_query, grad_keys, grad_values = pullback(grad_attended)
        grad_keys, grad_values = split_back(grad_keys), split_back(grad_values)
        grad_low = ADAPTER_SCALE * dot(grad_query, picked_up.astype(jnp.float32), ((1,), (1,)))
        return grad_query, grad_keys, grad_values, grad_low

    def project_in(grad, state, gradients):
        hidden, inverse, normed, low_rank, queries, keys, values, key_own, value_own = state
        grad_query, grad_keys, grad_values, grad_low = gradients
        back = (
            dot(grad_query.astype(jnp.bfloat16), query_weight, ((1,), (1,)))
            + dot(grad_keys.astype(jnp.bfloat16), key_weight, ((1,), (1,)))
            + dot(grad_values.astype(jnp.bfloat16), value_weight, ((1,), (1,)))
            + dot(grad_low, picked_down.astype(jnp.float32), ((1,), (1,)))
        )
        along = (
            jnp.sum(grad_query * queries, -1, keepdims=True)
            + jnp.sum(grad_keys * key_own, -1, keepdims=True)
            + jnp.sum(grad_values * value_own, -1, keepdims=True)
        ) / width
        stream = hidden.astype(jnp.float32)
        result = inverse * (back * gain) - stream * (inverse**2 * along)
        return (result + jnp.where(here, grad, 0).astype(jnp.float32)).astype(jnp.bfloat16)

    def travel(partial, start, end, ascending):
        pairs = [(a, b) for a in range(n) for b in range(n) if (a < b if ascending else a > b)]
        number = sum(jnp.where((start == a) & (end == b), i, 0) for i, (a, b) in enumerate(pairs))
        way = hop if n == 4 and nz <= FEW and local_rows % n == 0 else plain_hop
        return lax.switch(number, [lambda x, a=a, b=b: way(x, a, b) for a, b in pairs], partial)

    hidden = spread(tokens)

    def run(active):
        def branch(hidden):
            grad = spread(lax.optimization_barrier((cotangent, hidden))[0])
            state = forward(hidden)
            for j in range(1, active):
                got = travel(project_out(state), order[j - 1], order[j], True)
                state = forward(jnp.where(me == order[j], got, state[0]))
            gradients = backward(grad, state)
            for j in reversed(range(1, active)):
                got = travel(project_in(grad, state, gradients), order[j], order[j - 1], False)
                grad = jnp.where(me == order[j - 1], got, grad)
                gradients = backward(grad, state)
            grad_query, unused, unused, grad_low = gradients
            grad_up = ADAPTER_SCALE * dot(state[3], grad_query, ((0,), (0,)))
            grad_low = tensor_total(grad_low)
            mine = lax.dynamic_slice_in_dim(state[2], zi * piece_width, piece_width, 1)
            grad_down = dot(mine.astype(jnp.float32), grad_low, ((0,), (0,)))
            return grad_down, grad_up

        return branch

    grad_down, grad_up = lax.switch(count - 1, [run(active) for active in range(1, n)], hidden)
    return jnp.where(applies, grad_down, 0.0), jnp.where(applies, grad_up, 0.0)


def shards(
    tokens,
    cotangent,
    sequence_job,
    section_layer_list,
    section_norm_gain,
    query_matrix,
    key_matrix,
    value_matrix,
    output_matrix,
    adapter_down_all,
    adapter_up_all,
):
    n = lax.axis_size(S)
    gain = section_norm_gain[0].astype(jnp.float32)
    active = section_layer_list > 0
    rank = jnp.cumsum(active.astype(jnp.int32))
    order = [
        jnp.sum(jnp.where(active & (rank == j + 1), jnp.arange(n, dtype=jnp.int32), 0)) for j in range(n - 1)
    ]
    applies = jnp.sum(jnp.where(jnp.arange(n) == lax.axis_index(S), section_layer_list, 0)) > 0
    sections = (jnp.sum(active.astype(jnp.int32)), order, applies)
    weights = (query_matrix[0], key_matrix[0], value_matrix[0], output_matrix[0])
    adapters = (adapter_down_all[0], adapter_up_all[0])

    parts = [
        sequence_gradients(tokens[b], cotangent[b], sequence_job[b], sections, gain, weights, adapters)
        for b in range(tokens.shape[0])
    ]
    down = jnp.stack([p[0] for p in parts])
    up = jnp.stack([p[1] for p in parts])
    nd = lax.axis_size(D)
    downs, ups, jobs = [down], [up], [sequence_job]
    for r in range(1, nd):
        route = [(i, (i + r) % nd) for i in range(nd)]
        downs.append(lax.ppermute(down, D, route))
        ups.append(lax.ppermute(up, D, route))
        jobs.append(lax.ppermute(sequence_job, D, route))
    jobs = jnp.concatenate(jobs)
    wanted = (jobs[:, None] * ADAPTER_RANK + jnp.arange(ADAPTER_RANK, dtype=jnp.int32)[None, :]).reshape(-1, 1)
    place = (wanted == jnp.arange(ADAPTER_JOBS * ADAPTER_RANK, dtype=jnp.int32)[None, :]).astype(jnp.float32)
    downs = jnp.concatenate([x for block in downs for x in block], axis=1)
    ups = jnp.concatenate([x for block in ups for x in block], axis=0)
    grad_down = lax.dot_general(downs, place, (((1,), (0,)), ((), ())), precision=lax.Precision.HIGHEST)
    grad_up = lax.dot_general(place, ups, (((0,), (0,)), ((), ())), precision=lax.Precision.HIGHEST)
    return grad_down[None], grad_up[None]


def solution(mesh):
    in_specs = (
        P("dp", "tensor", None),
        P("dp", "tensor", None),
        P("dp"),
        P(),
        P("segment", None),
        P("segment", None, "tensor"),
        P("segment", None, "tensor"),
        P("segment", None, "tensor"),
        P("segment", "tensor", None),
        P("segment", "tensor", None),
        P("segment", None, "tensor"),
    )
    out_specs = (P("segment", "tensor", None), P("segment", None, "tensor"))
    return jax.shard_map(shards, mesh=mesh, in_specs=in_specs, out_specs=out_specs, check_vma=False)
```

```python
import itertools
import math

import jax
import jax.numpy as jnp
from jax import lax
from jax.experimental import pallas as pl
from jax.experimental.pallas import tpu as pltpu
from jax.sharding import PartitionSpec as P

HEAD_SIZE = 128
ADAPTER_RANK = 16
ADAPTER_JOBS = 32
ADAPTER_SCALE = 2.0
EPSILON = 1e-05

S, T, D = "segment", "tensor", "dp"
FEW = 4


def put(buffer, block, index):
    return lax.dynamic_update_slice_in_dim(buffer, block[None], index, 0)


def pick(stack, index):
    return lax.dynamic_index_in_dim(stack, index, 0, keepdims=False)


def rolled(block, columns, distance):
    nz = lax.axis_size(T)
    route = [(c * nz + z, c * nz + (z + distance) % nz) for c in columns for z in range(nz)]
    return lax.ppermute(block, (S, T), route)


def across(block, moves):
    nz = lax.axis_size(T)
    return lax.ppermute(block, (S, T), [(a * nz + z, b * nz + z) for a, b in moves for z in range(nz)])


def tensor_sum(stack, columns):
    nz, zi = lax.axis_size(T), lax.axis_index(T)
    total = pick(stack, zi).astype(jnp.float32)
    for r in range(1, nz):
        total = total + rolled(pick(stack, (zi + r) % nz), columns, r).astype(jnp.float32)
    return total.astype(stack.dtype)


def tensor_gather(block, columns):
    nz, zi = lax.axis_size(T), lax.axis_index(T)
    buffer = put(jnp.zeros((nz,) + block.shape, block.dtype), block, zi)
    for r in range(1, nz):
        buffer = put(buffer, rolled(block, columns, r), (zi - r) % nz)
    return buffer


def hop(partial, source, target):
    nz, me = lax.axis_size(T), lax.axis_index(S)
    rows, width = partial.shape
    groups = partial.reshape(nz, 4, rows // (4 * nz), width)
    to_x = across(groups[:, 2], [(source, source ^ 1)])
    to_y = across(groups[:, 3], [(source, source ^ 2)])
    own = tensor_sum(groups[:, 0:2], [source])
    one = tensor_sum(jnp.where(me == (source ^ 1), to_x, to_y), [source ^ 1, source ^ 2])
    if source ^ target == 3:
        by_x = across(jnp.where(me == source, own[1], one), [(source, target ^ 2), (target ^ 1, target)])
        by_y = across(jnp.where(me == source, own[0], one), [(source, target ^ 1), (target ^ 2, target)])
        pair = jnp.stack([by_y, by_x])
        single = jnp.where(me == (target ^ 2), by_x, by_y)
    else:
        rest = 3 - (source ^ target)
        got = across(jnp.where(me == source, own[1], one), [(source, target), (source ^ rest, target ^ rest)])
        pair = jnp.stack([got, one])
        single = jnp.where(me == source, own[0], got)
    gathered = tensor_gather(single, [target ^ 1, target ^ 2])
    from_x = across(gathered, [(target ^ 1, target)])
    from_y = across(gathered, [(target ^ 2, target)])
    two = tensor_gather(pair, [target])
    if source ^ target == 1:
        parts = [from_x, two[:, 0], two[:, 1], from_y]
    elif source ^ target == 2:
        parts = [from_y, two[:, 0], from_x, two[:, 1]]
    else:
        parts = [from_x, from_y, two[:, 0], two[:, 1]]
    return jnp.stack(parts, axis=1).reshape(rows, width)


def plain_hop(partial, source, target):
    shard = lax.psum_scatter(partial, T, scatter_dimension=0, tiled=True)
    shard = across(shard, [(source, target)])
    return lax.all_gather(shard, T, axis=0, tiled=True)


def built_of_permutes(width):
    return lax.axis_size(S) == 4 and lax.axis_size(T) == FEW and width % 2048 == 0


def spread_first(block):
    width = block.shape[1]
    if not built_of_permutes(width):
        return block
    unit = width // 16 * 3
    share = lax.dynamic_slice_in_dim(block, width - 4 * unit + lax.axis_index(S) * unit, unit, 1)
    return tensor_gather(share, range(4))


def spread_rest(block, mine):
    rows, width = block.shape
    if not built_of_permutes(width):
        return lax.all_gather(block, T, axis=0, tiled=True)
    nz, me = lax.axis_size(T), lax.axis_index(S)
    unit = mine.shape[2]
    first = width - 4 * unit
    half = nz // 2
    x_swap = [(c, c ^ 1) for c in range(4)]
    y_swap = [(c, c ^ 2) for c in range(4)]
    by_x = across(mine, x_swap)
    by_y = across(mine, y_swap)
    block, unused = lax.optimization_barrier((block, mine))
    base = tensor_gather(block[:, :first], range(4))
    far_low = across(by_y[:half], x_swap)
    far_high = across(by_x[half:], y_swap)
    out = jnp.zeros((nz, rows, width), block.dtype)
    out = lax.dynamic_update_slice(out, base, (0, 0, 0))
    for piece, column, z in (
        (mine, me, 0),
        (by_x, me ^ 1, 0),
        (by_y, me ^ 2, 0),
        (far_low, me ^ 3, 0),
        (far_high, me ^ 3, half),
    ):
        out = lax.dynamic_update_slice(out, piece, (z, 0, first + column * unit))
    return out.reshape(nz * rows, width)


def swapped(block, bit):
    count = lax.axis_size(T)
    return lax.ppermute(block, T, [(i, i ^ 1 << bit) for i in range(count)])


def tensor_total(block):
    nz = lax.axis_size(T)
    if nz & (nz - 1):
        return lax.psum(block, T)
    for bit in range(nz.bit_length() - 1):
        block = block + swapped(block, bit)
    return block


def rotation_tables(row_count):
    half_dim = HEAD_SIZE // 2
    positions = jnp.arange(row_count, dtype=jnp.float32)
    exponent = jnp.arange(half_dim, dtype=jnp.float32) * (2.0 / HEAD_SIZE)
    frequency = jnp.exp(-math.log(10000.0) * exponent)
    angles = positions[:, None] * frequency[None, :]
    cosine, sine = jnp.cos(angles), jnp.sin(angles)
    return jnp.concatenate([cosine, cosine], -1), jnp.concatenate([-sine, sine], -1)


def turned(x, cosine, sine):
    return x * cosine + pltpu.roll(x, HEAD_SIZE // 2, 1) * sine


def turned_back(x, cosine, sine):
    return x * cosine - pltpu.roll(x, HEAD_SIZE // 2, 1) * sine


def dot(a, b, dims=((1,), (0,))):
    return lax.dot_general(a, b, (dims, ((), ())), preferred_element_type=jnp.float32)


def head(ref, index):
    return ref[:, index * HEAD_SIZE : (index + 1) * HEAD_SIZE]


def head_weights(query, key):
    scores = dot(query, key, ((1,), (1,))) * (1.0 / math.sqrt(HEAD_SIZE))
    causal = lax.broadcasted_iota(jnp.int32, scores.shape, 0) >= lax.broadcasted_iota(jnp.int32, scores.shape, 1)
    weights = jnp.where(causal, jnp.exp(jnp.where(causal, scores, 0.0)), 0.0)
    return weights * (1.0 / jnp.sum(weights, axis=-1, keepdims=True))


def whole(shape):
    return pl.BlockSpec(shape, lambda i: (0,) * len(shape))


def tile_of(width):
    return math.gcd(width, 2048)


def call(kernel, steps, in_specs, out_specs, out_shape, scratch, flops, bytes_accessed):
    return pl.pallas_call(
        kernel,
        grid=(steps,),
        in_specs=in_specs,
        out_specs=out_specs,
        out_shape=out_shape,
        scratch_shapes=scratch,
        compiler_params=pltpu.CompilerParams(
            dimension_semantics=("arbitrary",), vmem_limit_bytes=56 * 2**20
        ),
        cost_estimate=pl.CostEstimate(flops=flops, bytes_accessed=bytes_accessed, transcendentals=0),
    )


def project_kernel(hidden, gain, query_w, key_w, value_w, down, up, queries, keys, values, low_rank, inverse):
    step = pl.program_id(0)
    tile = query_w.shape[0]

    @pl.when(step == 0)
    def _():
        squares = jnp.zeros((hidden.shape[0], 1), jnp.float32)
        for c in range(hidden.shape[1] // tile):
            part = hidden[:, c * tile : (c + 1) * tile].astype(jnp.float32)
            squares += jnp.sum(part * part, axis=-1, keepdims=True)
        inverse[...] = lax.rsqrt(squares * (1.0 / hidden.shape[1]) + EPSILON)
        for ref in (queries, keys, values, low_rank):
            ref[...] = jnp.zeros_like(ref)

    part = hidden[:, pl.ds(pl.multiple_of(step * tile, tile), tile)].astype(jnp.float32)
    normed = (part * inverse[...] * gain[...].astype(jnp.float32)).astype(jnp.bfloat16)
    queries[...] += dot(normed, query_w[...])
    keys[...] += dot(normed, key_w[...])
    values[...] += dot(normed, value_w[...])
    low_rank[...] += dot(normed, down[...], ((1,), (1,)))

    @pl.when(step == pl.num_programs(0) - 1)
    def _():
        queries[...] += ADAPTER_SCALE * dot(low_rank[...], up[...].astype(jnp.float32))


def project(hidden, gain, weights, down, up):
    query_w, key_w, value_w = weights
    rows, width = hidden.shape
    tile = tile_of(width)
    q, k = query_w.shape[1], key_w.shape[1]
    shapes = [(rows, q), (rows, k), (rows, k), (rows, ADAPTER_RANK), (rows, 1)]
    return call(
        project_kernel,
        width // tile,
        [
            whole((rows, width)),
            pl.BlockSpec((1, tile), lambda i: (0, i)),
            pl.BlockSpec((tile, q), lambda i: (i, 0)),
            pl.BlockSpec((tile, k), lambda i: (i, 0)),
            pl.BlockSpec((tile, k), lambda i: (i, 0)),
            pl.BlockSpec((ADAPTER_RANK, tile), lambda i: (0, i)),
            whole((ADAPTER_RANK, q)),
        ],
        [whole(shape) for shape in shapes],
        [jax.ShapeDtypeStruct(shape, jnp.float32) for shape in shapes],
        [],
        2 * rows * width * (q + 2 * k),
        2 * width * (rows + q + 2 * k),
    )(hidden, gain, query_w, key_w, value_w, down, up)


def output_kernel(queries, keys, values, cosine, sine, out_w, hidden, here, partial, attended):
    heads, key_heads = queries.shape[1] // HEAD_SIZE, keys.shape[1] // HEAD_SIZE

    @pl.when(pl.program_id(0) == 0)
    def _():
        for g in range(key_heads):
            key = turned(head(keys, g), cosine[...], sine[...]).astype(jnp.bfloat16)
            value = head(values, g).astype(jnp.bfloat16)
            for h in range(g * heads // key_heads, (g + 1) * heads // key_heads):
                query = turned(head(queries, h), cosine[...], sine[...]).astype(jnp.bfloat16)
                weights = head_weights(query, key).astype(jnp.bfloat16)
                attended[:, h * HEAD_SIZE : (h + 1) * HEAD_SIZE] = dot(weights, value).astype(jnp.bfloat16)

    result = dot(attended[...], out_w[...])
    partial[...] = (result + hidden[...].astype(jnp.float32) * here[...]).astype(jnp.bfloat16)


def output_partial(queries, keys, values, tables, out_w, hidden, here):
    rows, width = hidden.shape
    q = queries.shape[1]
    tile = tile_of(width)
    return call(
        output_kernel,
        width // tile,
        [
            whole(queries.shape),
            whole(keys.shape),
            whole(values.shape),
            whole(tables[0].shape),
            whole(tables[1].shape),
            pl.BlockSpec((q, tile), lambda i: (0, i)),
            pl.BlockSpec((rows, tile), lambda i: (0, i)),
            whole(here.shape),
        ],
        pl.BlockSpec((rows, tile), lambda i: (0, i)),
        jax.ShapeDtypeStruct((rows, width), jnp.bfloat16),
        [pltpu.VMEM((rows, q), jnp.bfloat16)],
        2 * rows * width * q,
        2 * width * (2 * rows + q),
    )(queries, keys, values, *tables, out_w, hidden, here)


def attend_back_kernel(
    grad, out_w, queries, keys, values, cosine, sine, low_rank, up,
    grad_query, grad_keys, grad_values, grad_low, grad_up, along, grad_attended,
):
    step = pl.program_id(0)
    heads, key_heads = queries.shape[1] // HEAD_SIZE, keys.shape[1] // HEAD_SIZE
    product = dot(grad[...], out_w[...], ((1,), (1,)))

    @pl.when(step == 0)
    def _():
        grad_attended[...] = product

    @pl.when(step > 0)
    def _():
        grad_attended[...] += product

    @pl.when(step == pl.num_programs(0) - 1)
    def _():
        scale = 1.0 / math.sqrt(HEAD_SIZE)
        along_sum = jnp.zeros(along.shape, jnp.float32)
        low_sum = jnp.zeros(grad_low.shape, jnp.float32)
        for g in range(key_heads):
            key = turned(head(keys, g), cosine[...], sine[...]).astype(jnp.bfloat16)
            value = head(values, g).astype(jnp.bfloat16)
            key_sum = jnp.zeros((keys.shape[0], HEAD_SIZE), jnp.float32)
            value_sum = jnp.zeros((keys.shape[0], HEAD_SIZE), jnp.float32)
            for h in range(g * heads // key_heads, (g + 1) * heads // key_heads):
                span = slice(h * HEAD_SIZE, (h + 1) * HEAD_SIZE)
                raw = queries[:, span]
                query = turned(raw, cosine[...], sine[...]).astype(jnp.bfloat16)
                weights = head_weights(query, key)
                back = grad_attended[:, span].astype(jnp.bfloat16)
                value_sum += dot(weights.astype(jnp.bfloat16), back, ((0,), (0,)))
                grad_weights = dot(back, value, ((1,), (1,)))
                mean = jnp.sum(grad_weights * weights, axis=-1, keepdims=True)
                grad_scores = (weights * (grad_weights - mean) * scale).astype(jnp.bfloat16)
                key_sum += dot(grad_scores, query, ((0,), (0,)))
                mine = turned_back(dot(grad_scores, key), cosine[...], sine[...])
                along_sum += jnp.sum(mine * raw, axis=-1, keepdims=True)
                up_part = up[:, span].astype(jnp.float32)
                low_sum += ADAPTER_SCALE * dot(mine, up_part, ((1,), (1,)))
                grad_up[:, span] = ADAPTER_SCALE * dot(low_rank[...], mine, ((0,), (0,)))
                grad_query[:, span] = mine.astype(jnp.bfloat16)
            grad_keys[:, g * HEAD_SIZE : (g + 1) * HEAD_SIZE] = turned_back(key_sum, cosine[...], sine[...])
            grad_values[:, g * HEAD_SIZE : (g + 1) * HEAD_SIZE] = value_sum
        along[...] = along_sum
        grad_low[...] = low_sum


def attend_back(grad, out_w, queries, keys, values, tables, low_rank, up):
    rows, width = grad.shape
    q = queries.shape[1]
    tile = tile_of(width)
    f32 = jnp.float32
    shapes = [
        ((rows, q), jnp.bfloat16),
        (keys.shape, f32),
        (values.shape, f32),
        ((rows, ADAPTER_RANK), f32),
        ((ADAPTER_RANK, q), f32),
        ((rows, 1), f32),
    ]
    return call(
        attend_back_kernel,
        width // tile,
        [
            pl.BlockSpec((rows, tile), lambda i: (0, i)),
            pl.BlockSpec((q, tile), lambda i: (0, i)),
            whole(queries.shape),
            whole(keys.shape),
            whole(values.shape),
            whole(tables[0].shape),
            whole(tables[1].shape),
            whole(low_rank.shape),
            whole(up.shape),
        ],
        [whole(shape) for shape, kind in shapes],
        [jax.ShapeDtypeStruct(shape, kind) for shape, kind in shapes],
        [pltpu.VMEM((rows, q), f32)],
        2 * rows * width * q,
        2 * width * (rows + q),
    )(grad, out_w, queries, keys, values, *tables, low_rank, up)


def input_kernel(
    grad_query, grad_keys, grad_values, grad_low, query_w, key_w, value_w, down, gain, inverse, along,
    hidden, grad, here, partial,
):
    across_last = ((1,), (1,))
    back = dot(grad_query[...], query_w[...], across_last)
    back += dot(grad_keys[...], key_w[...], across_last)
    back += dot(grad_values[...], value_w[...], across_last)
    back += dot(grad_low[...], down[...].astype(jnp.float32))
    result = back * gain[...].astype(jnp.float32) * inverse[...]
    result -= hidden[...].astype(jnp.float32) * along[...]
    partial[...] = (result + grad[...].astype(jnp.float32) * here[...]).astype(jnp.bfloat16)


def input_partial(grad_query, grad_keys, grad_values, grad_low, weights, down, gain, inverse, along, hidden, grad, here):
    query_w, key_w, value_w = weights
    rows, width = hidden.shape
    q, k = query_w.shape[1], key_w.shape[1]
    tile = tile_of(width)
    columns = pl.BlockSpec((rows, tile), lambda i: (0, i))
    return call(
        input_kernel,
        width // tile,
        [
            whole((rows, q)),
            whole((rows, k)),
            whole((rows, k)),
            whole((rows, ADAPTER_RANK)),
            pl.BlockSpec((tile, q), lambda i: (i, 0)),
            pl.BlockSpec((tile, k), lambda i: (i, 0)),
            pl.BlockSpec((tile, k), lambda i: (i, 0)),
            pl.BlockSpec((ADAPTER_RANK, tile), lambda i: (0, i)),
            pl.BlockSpec((1, tile), lambda i: (0, i)),
            whole((rows, 1)),
            whole((rows, 1)),
            columns,
            columns,
            whole((rows, 1)),
        ],
        columns,
        jax.ShapeDtypeStruct((rows, width), jnp.bfloat16),
        [],
        2 * rows * width * (q + 2 * k),
        2 * width * (3 * rows + q + 2 * k),
    )(grad_query, grad_keys, grad_values, grad_low, query_w, key_w, value_w, down, gain, inverse, along, hidden, grad, here)


def sequence_gradients(tokens, cotangent, job, sections, gain, weights, adapters):
    query_weight, key_weight, value_weight, out_weight = weights
    down_adapter, up_adapter = adapters
    n, nz = lax.axis_size(S), lax.axis_size(T)
    me, zi = lax.axis_index(S), lax.axis_index(T)
    local_rows, width = tokens.shape
    rows = local_rows * nz
    piece_width = down_adapter.shape[0]
    key_local = key_weight.shape[1]
    bits = (HEAD_SIZE // key_local).bit_length() - 1 if key_local < HEAD_SIZE else 0
    number, ways, applies = sections

    wanted = job * ADAPTER_RANK + jnp.arange(ADAPTER_RANK, dtype=jnp.int32)
    choice = (wanted[:, None] == jnp.arange(down_adapter.shape[1], dtype=jnp.int32)[None, :]).astype(jnp.bfloat16)
    picked_down = dot(choice, down_adapter, ((1,), (1,))).astype(jnp.bfloat16)
    picked_up = lax.dynamic_slice_in_dim(up_adapter, job * ADAPTER_RANK, ADAPTER_RANK, 0)
    here = (jnp.arange(rows) // local_rows == zi)[:, None].astype(jnp.float32)
    tables = rotation_tables(rows)

    def low_side(bit):
        return zi // 2**bit % 2 == 0

    def share_heads(block):
        for bit in range(bits):
            other = swapped(block.astype(jnp.bfloat16), bit).astype(block.dtype)
            block = jnp.where(
                low_side(bit), jnp.concatenate([block, other], -1), jnp.concatenate([other, block], -1)
            )
        return block

    def split_back(block):
        for bit in reversed(range(bits)):
            half = block.shape[-1] // 2
            keep = jnp.where(low_side(bit), block[:, :half], block[:, half:])
            send = jnp.where(low_side(bit), block[:, half:], block[:, :half])
            block = keep + swapped(send.astype(jnp.bfloat16), bit).astype(block.dtype)
        return block

    def forward(hidden):
        queries, keys, values, low_rank, inverse = project(hidden, gain, weights[:3], picked_down, picked_up)
        return hidden, inverse, low_rank, queries, share_heads(keys), share_heads(values), keys, values

    def project_out(state):
        hidden, unused, unused, queries, keys, values, unused, unused = state
        return output_partial(queries, keys, values, tables, out_weight, hidden, here)

    def backward(grad, state):
        hidden, inverse, low_rank, queries, keys, values, key_own, value_own = state
        grad_query, grad_keys, grad_values, grad_low, grad_up, along = attend_back(
            grad, out_weight, queries, keys, values, tables, low_rank, picked_up
        )
        return grad_query, split_back(grad_keys), split_back(grad_values), grad_low, grad_up, along

    def project_in(grad, state, gradients):
        hidden, inverse, low_rank, queries, keys, values, key_own, value_own = state
        grad_query, grad_keys, grad_values, grad_low, grad_up, along = gradients
        along += jnp.sum(grad_keys * key_own, -1, keepdims=True) + jnp.sum(grad_values * value_own, -1, keepdims=True)
        along *= inverse**2 / width
        grad_keys, grad_values = grad_keys.astype(jnp.bfloat16), grad_values.astype(jnp.bfloat16)
        return input_partial(
            grad_query, grad_keys, grad_values, grad_low, weights[:3], picked_down, gain, inverse, along, hidden, grad, here
        )

    def travel(partial, old, start, end):
        way = hop if built_of_permutes(width) and local_rows % n == 0 else plain_hop
        return jnp.where(me == end, way(partial, start, end), old)

    mine = spread_first(tokens)
    if nz == FEW:
        picked_down = tensor_gather(picked_down, range(n))
    else:
        picked_down = lax.all_gather(picked_down, T)
    picked_down = jnp.transpose(picked_down, (1, 0, 2)).reshape(ADAPTER_RANK, width)
    hidden = spread_rest(tokens, mine)

    def run(order):
        def branch(hidden):
            late, hidden = lax.optimization_barrier((cotangent, hidden))
            mine = spread_first(late)
            state = forward(hidden)
            mine, queries = lax.optimization_barrier((mine, state[3]))
            state = state[:3] + (queries,) + state[4:]
            grad = spread_rest(late, mine)
            for start, end in zip(order, order[1:]):
                partial, grad = lax.optimization_barrier((project_out(state), grad))
                state = forward(travel(partial, state[0], start, end))
            gradients = backward(grad, state)
            for end, start in reversed(list(zip(order, order[1:]))):
                grad = travel(project_in(grad, state, gradients), grad, start, end)
                gradients = backward(grad, state)
            grad_low, grad_up = gradients[3:5]
            grad_low = tensor_total(grad_low)
            mine = lax.dynamic_slice_in_dim(state[0], zi * piece_width, piece_width, 1).astype(jnp.float32)
            mine_gain = lax.dynamic_slice_in_dim(gain, zi * piece_width, piece_width, 1).astype(jnp.float32)
            normed = (mine * state[1] * mine_gain).astype(jnp.bfloat16)
            grad_down = dot(normed, grad_low.astype(jnp.bfloat16), ((0,), (0,)))
            return grad_down, grad_up

        return branch

    grad_down, grad_up = lax.switch(number, [run(order) for order in ways], hidden)
    return jnp.where(applies, grad_down, 0.0), jnp.where(applies, grad_up, 0.0)


def shards(
    tokens,
    cotangent,
    sequence_job,
    section_layer_list,
    section_norm_gain,
    query_matrix,
    key_matrix,
    value_matrix,
    output_matrix,
    adapter_down_all,
    adapter_up_all,
):
    n = lax.axis_size(S)
    gain = section_norm_gain
    active = section_layer_list > 0
    ways = [way for size in reversed(range(2, n)) for way in itertools.combinations(range(n), size)] + [(0,)]
    bits = jnp.sum(jnp.where(active, 2 ** jnp.arange(n, dtype=jnp.int32), 0))
    number = sum(
        jnp.where(bits == sum(2**section for section in way), i, 0) for i, way in enumerate(ways) if len(way) > 1
    )
    number = jnp.where(jnp.sum(active.astype(jnp.int32)) > 1, number, len(ways) - 1)
    applies = jnp.sum(jnp.where(jnp.arange(n) == lax.axis_index(S), section_layer_list, 0)) > 0
    sections = (number, ways, applies)
    weights = (query_matrix[0], key_matrix[0], value_matrix[0], output_matrix[0])
    adapters = (adapter_down_all[0], adapter_up_all[0])

    parts = [
        sequence_gradients(tokens[b], cotangent[b], sequence_job[b], sections, gain, weights, adapters)
        for b in range(tokens.shape[0])
    ]
    down = jnp.stack([p[0] for p in parts])
    up = jnp.stack([p[1] for p in parts])
    nd = lax.axis_size(D)
    jobs = jnp.broadcast_to(sequence_job[:, None, None].astype(jnp.float32), up.shape[:2] + (HEAD_SIZE,))
    sent = jnp.concatenate([jnp.swapaxes(down, 1, 2), up, jobs], axis=2)
    blocks = [sent] + [lax.ppermute(sent, D, [(i, (i + r) % nd) for i in range(nd)]) for r in range(1, nd)]
    blocks = jnp.concatenate(blocks)
    jobs = blocks[:, 0, -1].astype(jnp.int32)
    blocks = blocks.reshape(-1, blocks.shape[2])
    downs, ups = blocks[:, : down.shape[1]], blocks[:, down.shape[1] : -HEAD_SIZE]
    wanted = (jobs[:, None] * ADAPTER_RANK + jnp.arange(ADAPTER_RANK, dtype=jnp.int32)[None, :]).reshape(-1, 1)
    place = (wanted == jnp.arange(ADAPTER_JOBS * ADAPTER_RANK, dtype=jnp.int32)[None, :]).astype(jnp.float32)
    exact = lax.Precision.HIGHEST
    grad_down = lax.dot_general(downs, place, (((0,), (0,)), ((), ())), precision=exact)
    grad_up = lax.dot_general(place, ups, (((0,), (0,)), ((), ())), precision=exact)
    return grad_down[None], grad_up[None]


def solution(mesh):
    in_specs = (
        P("dp", "tensor", None),
        P("dp", "tensor", None),
        P("dp"),
        P(),
        P("segment", None),
        P("segment", None, "tensor"),
        P("segment", None, "tensor"),
        P("segment", None, "tensor"),
        P("segment", "tensor", None),
        P("segment", "tensor", None),
        P("segment", None, "tensor"),
    )
    out_specs = (P("segment", "tensor", None), P("segment", None, "tensor"))
    return jax.shard_map(shards, mesh=mesh, in_specs=in_specs, out_specs=out_specs, check_vma=False)
```

```python
import itertools
import math

import jax
import jax.numpy as jnp
from jax import lax
from jax.experimental import pallas as pl
from jax.experimental.pallas import tpu as pltpu
from jax.sharding import PartitionSpec as P

HEAD_SIZE = 128
ADAPTER_RANK = 16
ADAPTER_JOBS = 32
ADAPTER_SCALE = 2.0
EPSILON = 1e-05

S, T, D = "segment", "tensor", "dp"
FEW = 4


def put(buffer, block, index):
    return lax.dynamic_update_slice_in_dim(buffer, block[None], index, 0)


def pick(stack, index):
    return lax.dynamic_index_in_dim(stack, index, 0, keepdims=False)


def rolled(block, columns, distance):
    nz = lax.axis_size(T)
    route = [(c * nz + z, c * nz + (z + distance) % nz) for c in columns for z in range(nz)]
    return lax.ppermute(block, (S, T), route)


def across(block, moves):
    nz = lax.axis_size(T)
    return lax.ppermute(block, (S, T), [(a * nz + z, b * nz + z) for a, b in moves for z in range(nz)])


def tensor_sum(stack, columns):
    nz, zi = lax.axis_size(T), lax.axis_index(T)
    total = pick(stack, zi).astype(jnp.float32)
    for r in range(1, nz):
        total = total + rolled(pick(stack, (zi + r) % nz), columns, r).astype(jnp.float32)
    return total.astype(stack.dtype)


def tensor_gather(block, columns):
    nz, zi = lax.axis_size(T), lax.axis_index(T)
    buffer = put(jnp.zeros((nz,) + block.shape, block.dtype), block, zi)
    for r in range(1, nz):
        buffer = put(buffer, rolled(block, columns, r), (zi - r) % nz)
    return buffer


def hop(partial, source, target):
    nz, me = lax.axis_size(T), lax.axis_index(S)
    *kept, for_x, for_y = partial
    width = for_x.shape[1]
    rows = 4 * for_x.shape[0]
    part = rows // (4 * nz)
    own = kept[0].astype(jnp.float32)
    for r in range(1, nz):
        own = own + rolled(kept[r], [source], r).astype(jnp.float32)
    own = own.astype(jnp.bfloat16).reshape(2, part, width)
    to_x = across(for_x, [(source, source ^ 1)])
    to_y = across(for_y, [(source, source ^ 2)])
    to_one = jnp.where(me == (source ^ 1), to_x, to_y).reshape(nz, part, width)
    one = tensor_sum(to_one, [source ^ 1, source ^ 2])
    if source ^ target == 3:
        by_x = across(jnp.where(me == source, own[1], one), [(source, target ^ 2), (target ^ 1, target)])
        by_y = across(jnp.where(me == source, own[0], one), [(source, target ^ 1), (target ^ 2, target)])
        pair = jnp.stack([by_y, by_x])
        single = jnp.where(me == (target ^ 2), by_x, by_y)
    else:
        rest = 3 - (source ^ target)
        got = across(jnp.where(me == source, own[1], one), [(source, target), (source ^ rest, target ^ rest)])
        pair = jnp.stack([got, one])
        single = jnp.where(me == source, own[0], got)
    gathered = tensor_gather(single, [target ^ 1, target ^ 2])
    from_x = across(gathered, [(target ^ 1, target)])
    from_y = across(gathered, [(target ^ 2, target)])
    two = tensor_gather(pair, [target])
    if source ^ target == 1:
        parts = [from_x, two[:, 0], two[:, 1], from_y]
    elif source ^ target == 2:
        parts = [from_y, two[:, 0], from_x, two[:, 1]]
    else:
        parts = [from_x, from_y, two[:, 0], two[:, 1]]
    return jnp.stack(parts, axis=1).reshape(rows, width)


def plain_hop(partial, source, target):
    shard = lax.psum_scatter(partial, T, scatter_dimension=0, tiled=True)
    shard = across(shard, [(source, target)])
    return lax.all_gather(shard, T, axis=0, tiled=True)


def built_of_permutes(width):
    return lax.axis_size(S) == 4 and lax.axis_size(T) == FEW and width % 2048 == 0


def spread_first(block):
    width = block.shape[1]
    if not built_of_permutes(width):
        return block
    unit = width // 16 * 3
    share = lax.dynamic_slice_in_dim(block, width - 4 * unit + lax.axis_index(S) * unit, unit, 1)
    return tensor_gather(share, range(4))


def spread_next(mine, width):
    if not built_of_permutes(width):
        return mine
    by_x = across(mine, [(c, c ^ 1) for c in range(4)])
    by_y = across(mine, [(c, c ^ 2) for c in range(4)])
    return mine, by_x, by_y


def spread_base(block):
    width = block.shape[1]
    if not built_of_permutes(width):
        return block
    return tensor_gather(block[:, : width - 4 * (width // 16 * 3)], range(4))


def spread_last(block, state, base):
    rows, width = block.shape
    if not built_of_permutes(width):
        return lax.all_gather(block, T, axis=0, tiled=True)
    nz, me = lax.axis_size(T), lax.axis_index(S)
    mine, by_x, by_y = state
    unit = mine.shape[2]
    first = width - 4 * unit
    half = nz // 2
    far_low = across(by_y[:half], [(c, c ^ 1) for c in range(4)])
    far_high = across(by_x[half:], [(c, c ^ 2) for c in range(4)])
    out = jnp.zeros((nz, rows, width), block.dtype)
    out = lax.dynamic_update_slice(out, base, (0, 0, 0))
    for piece, column, z in (
        (mine, me, 0),
        (by_x, me ^ 1, 0),
        (by_y, me ^ 2, 0),
        (far_low, me ^ 3, 0),
        (far_high, me ^ 3, half),
    ):
        out = lax.dynamic_update_slice(out, piece, (z, 0, first + column * unit))
    return out.reshape(nz * rows, width)


def swapped(block, bit):
    count = lax.axis_size(T)
    return lax.ppermute(block, T, [(i, i ^ 1 << bit) for i in range(count)])


def tensor_total(block):
    nz = lax.axis_size(T)
    if nz > FEW:
        return lax.psum(block, T)
    return block + sum(rolled(block, range(lax.axis_size(S)), r) for r in range(1, nz))


def rotation_tables(row_count):
    half_dim = HEAD_SIZE // 2
    positions = jnp.arange(row_count, dtype=jnp.float32)
    exponent = jnp.arange(half_dim, dtype=jnp.float32) * (2.0 / HEAD_SIZE)
    frequency = jnp.exp(-math.log(10000.0) * exponent)
    angles = positions[:, None] * frequency[None, :]
    cosine, sine = jnp.cos(angles), jnp.sin(angles)
    return jnp.concatenate([cosine, cosine], -1), jnp.concatenate([-sine, sine], -1)


def turned(x, cosine, sine):
    return x * cosine + pltpu.roll(x, HEAD_SIZE // 2, 1) * sine


def turned_back(x, cosine, sine):
    return x * cosine - pltpu.roll(x, HEAD_SIZE // 2, 1) * sine


def dot(a, b, dims=((1,), (0,))):
    return lax.dot_general(a, b, (dims, ((), ())), preferred_element_type=jnp.float32)


def head(ref, index):
    return ref[:, index * HEAD_SIZE : (index + 1) * HEAD_SIZE]


def head_weights(query, key):
    scores = dot(query, key, ((1,), (1,))) * (1.0 / math.sqrt(HEAD_SIZE))
    causal = lax.broadcasted_iota(jnp.int32, scores.shape, 0) >= lax.broadcasted_iota(jnp.int32, scores.shape, 1)
    weights = jnp.where(causal, jnp.exp(jnp.where(causal, scores, 0.0)), 0.0)
    return weights * (1.0 / jnp.sum(weights, axis=-1, keepdims=True))


def whole(shape):
    return pl.BlockSpec(shape, lambda i: (0,) * len(shape))


def tile_of(width):
    return math.gcd(width, 2048)


def call(kernel, steps, in_specs, out_specs, out_shape, scratch, flops, bytes_accessed):
    return pl.pallas_call(
        kernel,
        grid=(steps,),
        in_specs=in_specs,
        out_specs=out_specs,
        out_shape=out_shape,
        scratch_shapes=scratch,
        compiler_params=pltpu.CompilerParams(
            dimension_semantics=("arbitrary",), vmem_limit_bytes=56 * 2**20
        ),
        cost_estimate=pl.CostEstimate(flops=flops, bytes_accessed=bytes_accessed, transcendentals=0),
    )


def project_kernel(hidden, gain, query_w, key_w, value_w, down, up, queries, keys, values, low_rank, inverse):
    step = pl.program_id(0)
    tile = query_w.shape[0]

    @pl.when(step == 0)
    def _():
        squares = jnp.zeros((hidden.shape[0], 1), jnp.float32)
        for c in range(hidden.shape[1] // tile):
            part = hidden[:, c * tile : (c + 1) * tile].astype(jnp.float32)
            squares += jnp.sum(part * part, axis=-1, keepdims=True)
        inverse[...] = lax.rsqrt(squares * (1.0 / hidden.shape[1]) + EPSILON)
        for ref in (queries, keys, values, low_rank):
            ref[...] = jnp.zeros_like(ref)

    part = hidden[:, pl.ds(pl.multiple_of(step * tile, tile), tile)].astype(jnp.float32)
    normed = (part * inverse[...] * gain[...].astype(jnp.float32)).astype(jnp.bfloat16)
    queries[...] += dot(normed, query_w[...])
    keys[...] += dot(normed, key_w[...])
    values[...] += dot(normed, value_w[...])
    low_rank[...] += dot(normed, down[...], ((1,), (1,)))

    @pl.when(step == pl.num_programs(0) - 1)
    def _():
        queries[...] += ADAPTER_SCALE * dot(low_rank[...], up[...].astype(jnp.float32))


def project(hidden, gain, weights, down, up):
    query_w, key_w, value_w = weights
    rows, width = hidden.shape
    tile = tile_of(width)
    q, k = query_w.shape[1], key_w.shape[1]
    shapes = [(rows, q), (rows, k), (rows, k), (rows, ADAPTER_RANK), (rows, 1)]
    return call(
        project_kernel,
        width // tile,
        [
            whole((rows, width)),
            pl.BlockSpec((1, tile), lambda i: (0, i)),
            pl.BlockSpec((tile, q), lambda i: (i, 0)),
            pl.BlockSpec((tile, k), lambda i: (i, 0)),
            pl.BlockSpec((tile, k), lambda i: (i, 0)),
            pl.BlockSpec((ADAPTER_RANK, tile), lambda i: (0, i)),
            whole((ADAPTER_RANK, q)),
        ],
        [whole(shape) for shape in shapes],
        [jax.ShapeDtypeStruct(shape, jnp.float32) for shape in shapes],
        [],
        2 * rows * width * (q + 2 * k),
        2 * width * (rows + q + 2 * k),
    )(hidden, gain, query_w, key_w, value_w, down, up)


def split_store(result, member, outs, whole_rows):
    if len(outs) == 1:
        outs[0][...] = result.astype(jnp.bfloat16)
        return
    *kept, for_x, for_y = outs
    whole_rows[...] = result.astype(jnp.bfloat16)
    nz, part = len(kept), kept[0].shape[0] // 2
    for r, ref in enumerate(kept):
        at = lax.rem(member[0] + r, nz) * (4 * part)
        ref[...] = whole_rows[pl.ds(pl.multiple_of(at, 4 * part), 2 * part), :]
    for z in range(nz):
        for_x[z * part : (z + 1) * part, :] = whole_rows[(4 * z + 2) * part : (4 * z + 3) * part, :]
        for_y[z * part : (z + 1) * part, :] = whole_rows[(4 * z + 3) * part : (4 * z + 4) * part, :]


def split_shapes(rows, width, split):
    if not split:
        heights = [rows]
    else:
        heights = [rows // (2 * FEW)] * FEW + [rows // 4] * 2
    tile = tile_of(width)
    specs = [pl.BlockSpec((height, tile), lambda i: (0, i)) for height in heights]
    return specs, [jax.ShapeDtypeStruct((height, width), jnp.bfloat16) for height in heights]


def output_kernel(member, queries, keys, values, cosine, sine, out_w, hidden, here, *rest):
    *outs, attended, whole_rows = rest
    heads, key_heads = queries.shape[1] // HEAD_SIZE, keys.shape[1] // HEAD_SIZE

    @pl.when(pl.program_id(0) == 0)
    def _():
        for g in range(key_heads):
            key = turned(head(keys, g), cosine[...], sine[...]).astype(jnp.bfloat16)
            value = head(values, g).astype(jnp.bfloat16)
            for h in range(g * heads // key_heads, (g + 1) * heads // key_heads):
                query = turned(head(queries, h), cosine[...], sine[...]).astype(jnp.bfloat16)
                weights = head_weights(query, key).astype(jnp.bfloat16)
                attended[:, h * HEAD_SIZE : (h + 1) * HEAD_SIZE] = dot(weights, value).astype(jnp.bfloat16)

    result = dot(attended[...], out_w[...])
    split_store(result + hidden[...].astype(jnp.float32) * here[...], member, outs, whole_rows)


def output_partial(member, queries, keys, values, tables, out_w, hidden, here, split):
    rows, width = hidden.shape
    q = queries.shape[1]
    tile = tile_of(width)
    specs, out_shape = split_shapes(rows, width, split)
    return call(
        output_kernel,
        width // tile,
        [
            pl.BlockSpec(memory_space=pltpu.SMEM),
            whole(queries.shape),
            whole(keys.shape),
            whole(values.shape),
            whole(tables[0].shape),
            whole(tables[1].shape),
            pl.BlockSpec((q, tile), lambda i: (0, i)),
            pl.BlockSpec((rows, tile), lambda i: (0, i)),
            whole(here.shape),
        ],
        specs,
        out_shape,
        [pltpu.VMEM((rows, q), jnp.bfloat16), pltpu.VMEM((rows, tile), jnp.bfloat16)],
        2 * rows * width * q,
        2 * width * (2 * rows + q),
    )(member, queries, keys, values, *tables, out_w, hidden, here)


def attend_back_kernel(
    grad, out_w, queries, keys, values, cosine, sine, low_rank, up,
    grad_query, grad_keys, grad_values, grad_low, grad_up, along, grad_attended,
):
    step = pl.program_id(0)
    heads, key_heads = queries.shape[1] // HEAD_SIZE, keys.shape[1] // HEAD_SIZE
    product = dot(grad[...], out_w[...], ((1,), (1,)))

    @pl.when(step == 0)
    def _():
        grad_attended[...] = product

    @pl.when(step > 0)
    def _():
        grad_attended[...] += product

    @pl.when(step == pl.num_programs(0) - 1)
    def _():
        scale = 1.0 / math.sqrt(HEAD_SIZE)
        along_sum = jnp.zeros(along.shape, jnp.float32)
        low_sum = jnp.zeros(grad_low.shape, jnp.float32)
        for g in range(key_heads):
            key = turned(head(keys, g), cosine[...], sine[...]).astype(jnp.bfloat16)
            value = head(values, g).astype(jnp.bfloat16)
            key_sum = jnp.zeros((keys.shape[0], HEAD_SIZE), jnp.float32)
            value_sum = jnp.zeros((keys.shape[0], HEAD_SIZE), jnp.float32)
            for h in range(g * heads // key_heads, (g + 1) * heads // key_heads):
                span = slice(h * HEAD_SIZE, (h + 1) * HEAD_SIZE)
                raw = queries[:, span]
                query = turned(raw, cosine[...], sine[...]).astype(jnp.bfloat16)
                weights = head_weights(query, key)
                back = grad_attended[:, span].astype(jnp.bfloat16)
                value_sum += dot(weights.astype(jnp.bfloat16), back, ((0,), (0,)))
                grad_weights = dot(back, value, ((1,), (1,)))
                mean = jnp.sum(grad_weights * weights, axis=-1, keepdims=True)
                grad_scores = (weights * (grad_weights - mean) * scale).astype(jnp.bfloat16)
                key_sum += dot(grad_scores, query, ((0,), (0,)))
                mine = turned_back(dot(grad_scores, key), cosine[...], sine[...])
                along_sum += jnp.sum(mine * raw, axis=-1, keepdims=True)
                up_part = up[:, span].astype(jnp.float32)
                low_sum += ADAPTER_SCALE * dot(mine, up_part, ((1,), (1,)))
                grad_up[:, span] = ADAPTER_SCALE * dot(low_rank[...], mine, ((0,), (0,)))
                grad_query[:, span] = mine.astype(jnp.bfloat16)
            grad_keys[:, g * HEAD_SIZE : (g + 1) * HEAD_SIZE] = turned_back(key_sum, cosine[...], sine[...])
            grad_values[:, g * HEAD_SIZE : (g + 1) * HEAD_SIZE] = value_sum
        along[...] = along_sum
        grad_low[...] = low_sum


def attend_back(grad, out_w, queries, keys, values, tables, low_rank, up):
    rows, width = grad.shape
    q = queries.shape[1]
    tile = tile_of(width)
    f32 = jnp.float32
    shapes = [
        ((rows, q), jnp.bfloat16),
        (keys.shape, f32),
        (values.shape, f32),
        ((rows, ADAPTER_RANK), f32),
        ((ADAPTER_RANK, q), f32),
        ((rows, 1), f32),
    ]
    return call(
        attend_back_kernel,
        width // tile,
        [
            pl.BlockSpec((rows, tile), lambda i: (0, i)),
            pl.BlockSpec((q, tile), lambda i: (0, i)),
            whole(queries.shape),
            whole(keys.shape),
            whole(values.shape),
            whole(tables[0].shape),
            whole(tables[1].shape),
            whole(low_rank.shape),
            whole(up.shape),
        ],
        [whole(shape) for shape, kind in shapes],
        [jax.ShapeDtypeStruct(shape, kind) for shape, kind in shapes],
        [pltpu.VMEM((rows, q), f32)],
        2 * rows * width * q,
        2 * width * (rows + q),
    )(grad, out_w, queries, keys, values, *tables, low_rank, up)


def input_kernel(
    member, grad_query, grad_keys, grad_values, grad_low, query_w, key_w, value_w, down, gain, inverse, along,
    hidden, grad, here, *rest,
):
    *outs, whole_rows = rest
    across_last = ((1,), (1,))
    back = dot(grad_query[...], query_w[...], across_last)
    back += dot(grad_keys[...], key_w[...], across_last)
    back += dot(grad_values[...], value_w[...], across_last)
    back += dot(grad_low[...], down[...].astype(jnp.float32))
    result = back * gain[...].astype(jnp.float32) * inverse[...]
    result -= hidden[...].astype(jnp.float32) * along[...]
    split_store(result + grad[...].astype(jnp.float32) * here[...], member, outs, whole_rows)


def input_partial(
    member, grad_query, grad_keys, grad_values, grad_low, weights, down, gain, inverse, along, hidden, grad, here, split
):
    query_w, key_w, value_w = weights
    rows, width = hidden.shape
    q, k = query_w.shape[1], key_w.shape[1]
    tile = tile_of(width)
    columns = pl.BlockSpec((rows, tile), lambda i: (0, i))
    specs, out_shape = split_shapes(rows, width, split)
    return call(
        input_kernel,
        width // tile,
        [
            pl.BlockSpec(memory_space=pltpu.SMEM),
            whole((rows, q)),
            whole((rows, k)),
            whole((rows, k)),
            whole((rows, ADAPTER_RANK)),
            pl.BlockSpec((tile, q), lambda i: (i, 0)),
            pl.BlockSpec((tile, k), lambda i: (i, 0)),
            pl.BlockSpec((tile, k), lambda i: (i, 0)),
            pl.BlockSpec((ADAPTER_RANK, tile), lambda i: (0, i)),
            pl.BlockSpec((1, tile), lambda i: (0, i)),
            whole((rows, 1)),
            whole((rows, 1)),
            columns,
            columns,
            whole((rows, 1)),
        ],
        specs,
        out_shape,
        [pltpu.VMEM((rows, tile), jnp.bfloat16)],
        2 * rows * width * (q + 2 * k),
        2 * width * (3 * rows + q + 2 * k),
    )(
        member, grad_query, grad_keys, grad_values, grad_low, query_w, key_w, value_w, down, gain, inverse, along,
        hidden, grad, here,
    )


def sequence_gradients(tokens, cotangent, job, sections, gain, weights, adapters):
    query_weight, key_weight, value_weight, out_weight = weights
    down_adapter, up_adapter = adapters
    n, nz = lax.axis_size(S), lax.axis_size(T)
    me, zi = lax.axis_index(S), lax.axis_index(T)
    local_rows, width = tokens.shape
    rows = local_rows * nz
    piece_width = down_adapter.shape[0]
    key_local = key_weight.shape[1]
    bits = (HEAD_SIZE // key_local).bit_length() - 1 if key_local < HEAD_SIZE else 0
    number, ways, applies = sections

    wanted = job * ADAPTER_RANK + jnp.arange(ADAPTER_RANK, dtype=jnp.int32)
    choice = (wanted[:, None] == jnp.arange(down_adapter.shape[1], dtype=jnp.int32)[None, :]).astype(jnp.bfloat16)
    picked_down = dot(choice, down_adapter, ((1,), (1,))).astype(jnp.bfloat16)
    picked_up = lax.dynamic_slice_in_dim(up_adapter, job * ADAPTER_RANK, ADAPTER_RANK, 0)
    split = built_of_permutes(width) and local_rows % (16 * n) == 0
    member = jnp.reshape(zi, (1,)).astype(jnp.int32)
    here = (jnp.arange(rows) // local_rows == zi)[:, None].astype(jnp.float32)
    tables = rotation_tables(rows)

    def low_side(bit):
        return zi // 2**bit % 2 == 0

    def share_heads(block):
        for bit in range(bits):
            other = swapped(block.astype(jnp.bfloat16), bit).astype(block.dtype)
            block = jnp.where(
                low_side(bit), jnp.concatenate([block, other], -1), jnp.concatenate([other, block], -1)
            )
        return block

    def split_back(block):
        for bit in reversed(range(bits)):
            half = block.shape[-1] // 2
            keep = jnp.where(low_side(bit), block[:, :half], block[:, half:])
            send = jnp.where(low_side(bit), block[:, half:], block[:, :half])
            block = keep + swapped(send.astype(jnp.bfloat16), bit).astype(block.dtype)
        return block

    def forward(hidden):
        queries, keys, values, low_rank, inverse = project(hidden, gain, weights[:3], picked_down, picked_up)
        return hidden, inverse, low_rank, queries, share_heads(keys), share_heads(values), keys, values

    def project_out(state):
        hidden, unused, unused, queries, keys, values, unused, unused = state
        return output_partial(member, queries, keys, values, tables, out_weight, hidden, here, split)

    def backward(grad, state):
        hidden, inverse, low_rank, queries, keys, values, key_own, value_own = state
        grad_query, grad_keys, grad_values, grad_low, grad_up, along = attend_back(
            grad, out_weight, queries, keys, values, tables, low_rank, picked_up
        )
        return grad_query, split_back(grad_keys), split_back(grad_values), grad_low, grad_up, along

    def project_in(grad, state, gradients):
        hidden, inverse, low_rank, queries, keys, values, key_own, value_own = state
        grad_query, grad_keys, grad_values, grad_low, grad_up, along = gradients
        along += jnp.sum(grad_keys * key_own, -1, keepdims=True) + jnp.sum(grad_values * value_own, -1, keepdims=True)
        along *= inverse**2 / width
        grad_keys, grad_values = grad_keys.astype(jnp.bfloat16), grad_values.astype(jnp.bfloat16)
        return input_partial(
            member, grad_query, grad_keys, grad_values, grad_low, weights[:3], picked_down, gain, inverse, along,
            hidden, grad, here, split,
        )

    def travel(partial, old, start, end):
        got = hop(partial, start, end) if split else plain_hop(partial[0], start, end)
        return jnp.where(me == end, got, old)

    mine, late_tokens = lax.optimization_barrier((spread_first(tokens), tokens))
    swap, base = spread_next(mine, width), spread_base(late_tokens)
    late_down, swap = lax.optimization_barrier((picked_down, swap))
    hidden = spread_last(tokens, swap, base)
    if nz == FEW:
        picked_down = tensor_gather(late_down, range(n))
    else:
        picked_down = lax.all_gather(late_down, T)
    picked_down = jnp.transpose(picked_down, (1, 0, 2)).reshape(ADAPTER_RANK, width)

    def run(order):
        def branch(hidden):
            late, hidden = lax.optimization_barrier((cotangent, hidden))
            mine = spread_first(late)
            state = forward(hidden)
            mine, late, queries = lax.optimization_barrier((mine, late, state[3]))
            state = state[:3] + (queries,) + state[4:]
            swap = spread_next(mine, width)
            for number, (start, end) in enumerate(zip(order, order[1:])):
                partial = project_out(state)
                if number == 0:
                    partial, swap = lax.optimization_barrier((partial, swap))
                hidden = travel(partial, state[0], start, end)
                if number == 0:
                    late, swap, hidden = lax.optimization_barrier((late, swap, hidden))
                state = forward(hidden)
            grad = spread_last(late, swap, spread_base(late))
            gradients = backward(grad, state)
            for end, start in reversed(list(zip(order, order[1:]))):
                grad = travel(project_in(grad, state, gradients), grad, start, end)
                gradients = backward(grad, state)
            grad_low, grad_up = gradients[3:5]
            grad_low = tensor_total(grad_low)
            mine = lax.dynamic_slice_in_dim(state[0], zi * piece_width, piece_width, 1).astype(jnp.float32)
            mine_gain = lax.dynamic_slice_in_dim(gain, zi * piece_width, piece_width, 1).astype(jnp.float32)
            normed = (mine * state[1] * mine_gain).astype(jnp.bfloat16)
            grad_down = dot(normed, grad_low.astype(jnp.bfloat16), ((0,), (0,)))
            return grad_down, grad_up

        return branch

    grad_down, grad_up = lax.switch(number, [run(order) for order in ways], hidden)
    return jnp.where(applies, grad_down, 0.0), jnp.where(applies, grad_up, 0.0)


def shards(
    tokens,
    cotangent,
    sequence_job,
    section_layer_list,
    section_norm_gain,
    query_matrix,
    key_matrix,
    value_matrix,
    output_matrix,
    adapter_down_all,
    adapter_up_all,
):
    n = lax.axis_size(S)
    gain = section_norm_gain
    active = section_layer_list > 0
    ways = [(0,)] + [way for size in range(2, n) for way in itertools.combinations(range(n), size)]
    bits = jnp.sum(jnp.where(active, 2 ** jnp.arange(n, dtype=jnp.int32), 0))
    number = sum(
        jnp.where(bits == sum(2**section for section in way), i, 0) for i, way in enumerate(ways) if len(way) > 1
    )
    applies = jnp.sum(jnp.where(jnp.arange(n) == lax.axis_index(S), section_layer_list, 0)) > 0
    sections = (number, ways, applies)
    weights = (query_matrix[0], key_matrix[0], value_matrix[0], output_matrix[0])
    adapters = (adapter_down_all[0], adapter_up_all[0])

    parts = [
        sequence_gradients(tokens[b], cotangent[b], sequence_job[b], sections, gain, weights, adapters)
        for b in range(tokens.shape[0])
    ]
    down = jnp.stack([p[0] for p in parts])
    up = jnp.stack([p[1] for p in parts])
    nd = lax.axis_size(D)
    jobs = jnp.broadcast_to(sequence_job[:, None, None].astype(jnp.float32), up.shape[:2] + (HEAD_SIZE,))
    sent = jnp.concatenate([jnp.swapaxes(down, 1, 2), up, jobs], axis=2)
    blocks = [sent] + [lax.ppermute(sent, D, [(i, (i + r) % nd) for i in range(nd)]) for r in range(1, nd)]
    blocks = jnp.concatenate(blocks)
    jobs = blocks[:, 0, -1].astype(jnp.int32)
    blocks = blocks.reshape(-1, blocks.shape[2])
    downs, ups = blocks[:, : down.shape[1]], blocks[:, down.shape[1] : -HEAD_SIZE]
    wanted = (jobs[:, None] * ADAPTER_RANK + jnp.arange(ADAPTER_RANK, dtype=jnp.int32)[None, :]).reshape(-1, 1)
    place = (wanted == jnp.arange(ADAPTER_JOBS * ADAPTER_RANK, dtype=jnp.int32)[None, :]).astype(jnp.float32)
    exact = lax.Precision.HIGHEST
    grad_down = lax.dot_general(downs, place, (((0,), (0,)), ((), ())), precision=exact)
    grad_up = lax.dot_general(place, ups, (((0,), (0,)), ((), ())), precision=exact)
    return grad_down[None], grad_up[None]


def solution(mesh):
    in_specs = (
        P("dp", "tensor", None),
        P("dp", "tensor", None),
        P("dp"),
        P(),
        P("segment", None),
        P("segment", None, "tensor"),
        P("segment", None, "tensor"),
        P("segment", None, "tensor"),
        P("segment", "tensor", None),
        P("segment", "tensor", None),
        P("segment", None, "tensor"),
    )
    out_specs = (P("segment", "tensor", None), P("segment", None, "tensor"))
    return jax.shard_map(shards, mesh=mesh, in_specs=in_specs, out_specs=out_specs, check_vma=False)
```
